32 devices in a mesh: orig: 8 (over z, y), dest: 4 (over x, core).
Axes of the slice: x: 2, y: 2, z: 4, core: 2. Of those that a mesh axis runs over, the one named last changes fastest.
Arguments:
- skim_tables: bfloat16 [8, 8192, 8192], P(None, 'orig', 'dest'), may hold values from 0 to 4
- block_scale: float32 [8, 64, 64], P(None, 'orig', 'dest'), may hold values from 0.25 to 60
- mode_coef: float32 [12, 8], replicated, may hold values from -1.2 to 1.2
- mode_const: float32 [12], replicated, may hold values from -4 to 4
- nest_theta: float32 [4], replicated, may hold values from 0.3 to 1
- mode_nest: int32 [12], replicated, may hold values from 0 to 3, as said below
- logsum_coef: float32 [1], replicated, may hold values from 0.5 to 1
- tour_attr: bfloat16 [32768, 128], P('orig')
- zone_attr: bfloat16 [128, 8192], P(None, 'dest')
- block_zone: int32 [1024], P('orig'), may hold values from 0 to 8191, as said below
- block_count: int32 [1024], P('orig'), may hold values from 1 to 32, as said below
Outputs:
- logsums: float32 [8192, 8192], P('orig', 'dest')
- trip_matrix: float32 [8192, 8192], P('orig', 'dest')
The draws below stay inside these ranges and needn't reach their ends.
Inputs may be any that keep to these rules, and one draw needn't show every extreme that they name: `block_zone`: among the 128 blocks of each aligned run (the blocks of one index of orig), at most 32 have home zones in any one range of 1024 zones (zone // 1024); one range has exactly 32 blocks in every run. `block_count`: each aligned run of 128 blocks has a block with 32 live tours. `mode_nest`: every nest holds at least one mode.
All inputs are finite; a program needn't handle non-finite values.
Results may differ from the reference program's by a relative error of at most 0.0006.
Values may be sent and summed in bfloat16 or wider, within the bound.
A program may use at most 384 MiB of HBM per device.

```python
import math
import jax
import jax.numpy as jnp
from jax import lax

Z = 8192
MODES = 12
TABLES = 8
NESTS = 4
F = 128
SB = 128
TB = 32
NBD = 128
ZO = 1024
CAP = 32
NB = 1024
TOURS = 32768


def draw_block_scale(key, part):
    groups = Z // SB
    base = jax.random.uniform(jax.random.fold_in(key, 21), (TABLES, groups, groups), jnp.float32)
    scale = 0.25 * jnp.exp(base * jnp.log(8.0))
    return scale


def draw_mode_nest(key, part):
    order = jax.random.permutation(jax.random.fold_in(key, 31), MODES)
    extra = jax.random.randint(jax.random.fold_in(key, 32), (MODES,), 0, NESTS)
    return jnp.where(order < NESTS, order, extra).astype(jnp.int32)


def zone_base(key):
    return jax.random.normal(jax.random.fold_in(key, 41), (F, Z), jnp.float32) * F ** (-0.5)


def draw_zone_attr(key, part):
    return zone_base(key).astype(jnp.bfloat16)


def draw_tour_attr(key, part):
    drawn = 2.5 * jax.random.normal(jax.random.fold_in(key, 51), (TOURS, F), jnp.float32)
    return drawn.astype(jnp.bfloat16)


def draw_block_zone(key, part):
    sources = NB // NBD
    heavy = jax.random.randint(jax.random.fold_in(key, 61), (), 0, sources)
    pool = jnp.arange((sources - 1) * CAP) // CAP
    pool = pool + (pool >= heavy).astype(jnp.int32)

    def one_device(index):
        device_key = jax.random.fold_in(jax.random.fold_in(key, 62), index)
        order = jax.random.permutation(jax.random.fold_in(device_key, 1), (sources - 1) * CAP)
        picked = pool[order[:NBD - CAP]].astype(jnp.int32)
        chosen = jnp.concatenate([jnp.full((CAP,), heavy, jnp.int32), picked])
        mixed = chosen[jax.random.permutation(jax.random.fold_in(device_key, 2), NBD)]
        local_zone = jax.random.randint(jax.random.fold_in(device_key, 3), (NBD,), 0, ZO)
        return mixed * ZO + local_zone
    return jax.vmap(one_device)(jnp.arange(sources)).reshape(NB).astype(jnp.int32)


def draw_block_count(key, part):
    sources = NB // NBD
    counts = jax.random.randint(jax.random.fold_in(key, 71), (sources, NBD), 1, TB + 1)
    full_at = jax.random.randint(jax.random.fold_in(key, 72), (sources, 1), 0, NBD)
    return jnp.where(jnp.arange(NBD)[None, :] == full_at, TB, counts).reshape(NB).astype(jnp.int32)


def steps_of(own_key, shape, shards, smallest, high):
    factor_of, own = 1.0, jax.random.fold_in(own_key, 6)
    for position, shards_of in shards:
        draws = jnp.exp(jax.random.uniform(jax.random.fold_in(own, position), (shards_of,), jnp.float32, smallest / len(shards), high / len(shards)))
        factor_of = factor_of * jnp.repeat(draws, shape[position] // shards_of).reshape([-1 if axis == position else 1 for axis in range(len(shape))])
    return factor_of


def noise(rng, dims, deviation, bound, kind=jnp.bfloat16):
    result = deviation * jax.random.normal(rng, dims, jnp.float32)
    return jnp.clip(result, min=-bound, max=bound).astype(kind)


def setup_inputs(seed: int = 0) -> dict:
    streams_of = jax.random.split(jax.random.key(seed), 12)
    skim_tables = jnp.clip(4.0 * jax.random.uniform(streams_of[0], (TABLES, Z, Z), jnp.float32) ** steps_of(streams_of[0], (TABLES, Z, Z), ((1, 8), (2, 4)), -0.2, 0.2), 0.0, 4.0).astype(jnp.bfloat16)
    block_scale = draw_block_scale(jax.random.fold_in(streams_of[11], 71), 0)
    mode_coef = noise(streams_of[2], (MODES, TABLES), 0.3, 1.2, jnp.float32)
    mode_const = noise(streams_of[3], (MODES,), 1.0, 4.0, jnp.float32)
    nest_theta = jnp.clip(jnp.exp(jax.random.uniform(streams_of[4], (NESTS,), jnp.float32, math.log(0.3), math.log(1.0))), 0.3, 1.0)
    mode_nest = draw_mode_nest(jax.random.fold_in(streams_of[11], 71), 0)
    logsum_coef = jnp.clip(jax.random.uniform(streams_of[6], (1,), jnp.float32, 0.5, 1.0), 0.5, 1.0)
    tour_attr = draw_tour_attr(jax.random.fold_in(streams_of[11], 71), 0)
    zone_attr = draw_zone_attr(jax.random.fold_in(streams_of[11], 71), 0)
    block_zone = draw_block_zone(jax.random.fold_in(streams_of[11], 71), 0)
    block_count = draw_block_count(jax.random.fold_in(streams_of[11], 71), 0)
    return dict(skim_tables=skim_tables, block_scale=block_scale, mode_coef=mode_coef, mode_const=mode_const, nest_theta=nest_theta, mode_nest=mode_nest, logsum_coef=logsum_coef, tour_attr=tour_attr, zone_attr=zone_attr, block_zone=block_zone, block_count=block_count)


neg_fill = -1.0e30


def nest_logsum(skim_part, scale_part, mode_coef, mode_const, nest_theta, mode_nest):
    tables, row_count, col_count = skim_part.shape
    block_rows = row_count // scale_part.shape[1]
    block_cols = col_count // scale_part.shape[2]
    nest_total = nest_theta.shape[0]
    mode_total = mode_coef.shape[0]
    scaled = skim_part.astype(jnp.float32).reshape(tables, scale_part.shape[1], block_rows, scale_part.shape[2], block_cols)
    scaled = (scaled * scale_part[:, :, None, :, None]).reshape(tables, row_count, col_count)
    member_table = mode_nest[:, None] == jnp.arange(nest_total, dtype=jnp.int32)[None, :]
    mode_theta = jnp.sum(jnp.where(member_table, nest_theta[None, :], jnp.float32(0.0)), axis=1)
    utils = []
    for mode_index in range(mode_total):
        value = mode_const[mode_index] + mode_coef[mode_index, 0] * scaled[0]
        for table_index in range(1, tables):
            value = value + mode_coef[mode_index, table_index] * scaled[table_index]
        utils.append(value / mode_theta[mode_index])
    scaled_util = jnp.stack(utils)
    maxima = []
    for nest_index in range(nest_total):
        member = (mode_nest == nest_index)[:, None, None]
        maxima.append(jnp.max(jnp.where(member, scaled_util, neg_fill), axis=0))
    nest_values = []
    for nest_index in range(nest_total):
        member = (mode_nest == nest_index)[:, None, None]
        shifted = jnp.where(member, scaled_util - maxima[nest_index][None], neg_fill)
        sum_total = jnp.sum(jnp.exp(shifted), axis=0)
        nest_values.append(nest_theta[nest_index] * (maxima[nest_index] + jnp.log(sum_total)))
    stacked = jnp.stack(nest_values)
    row_max = jnp.max(stacked, axis=0)
    return row_max + jnp.log(jnp.sum(jnp.exp(stacked - row_max), axis=0))


def reference(skim_tables, block_scale, mode_coef, mode_const, nest_theta, mode_nest, logsum_coef, tour_attr, zone_attr, block_zone, block_count):
    anchor_groups = Z // SB

    def anchor_rows(index):
        start = (index * SB).astype(jnp.int32)
        skim_part = lax.dynamic_slice_in_dim(skim_tables, start, SB, 1)
        scale_part = lax.dynamic_slice_in_dim(block_scale, index.astype(jnp.int32), 1, 1)
        return nest_logsum(skim_part, scale_part, mode_coef, mode_const, nest_theta, mode_nest)

    logsums = lax.map(anchor_rows, jnp.arange(anchor_groups, dtype=jnp.int32)).reshape(Z, Z)
    total_blocks = block_zone.shape[0]
    group_size = math.gcd(total_blocks, max(1, 512 // TB))
    grouped_feats = tour_attr.reshape(total_blocks // group_size, group_size * TB, F)
    grouped_zones = block_zone.reshape(-1, group_size)
    grouped_counts = block_count.reshape(-1, group_size)
    zone_wide = zone_attr.astype(jnp.float32)
    ls_coef = logsum_coef[0]

    def group_trips(inputs):
        feat_part, zone_part, count_part = inputs
        home_rows = logsums[zone_part]
        product = jnp.dot(feat_part.astype(jnp.float32), zone_wide, preferred_element_type=jnp.float32)
        scores = ls_coef * home_rows[:, None, :] + product.reshape(group_size, TB, Z)
        row_max = jnp.max(scores, axis=-1, keepdims=True)
        weights = jnp.exp(scores - row_max)
        shares = weights / jnp.sum(weights, axis=-1, keepdims=True)
        live_mask = (jnp.arange(TB)[None, :] < count_part[:, None]).astype(jnp.float32)
        return jnp.sum(shares * live_mask[:, :, None], axis=1)

    block_sums = lax.map(group_trips, (grouped_feats, grouped_zones, grouped_counts)).reshape(total_blocks, Z)
    trip_matrix = (Z / TB) * jax.ops.segment_sum(block_sums, block_zone, num_segments=Z)
    return logsums, trip_matrix
```

```python
import functools
import math

import jax
import jax.numpy as jnp
from jax import lax
from jax.experimental import pallas as pl
from jax.experimental.pallas import tpu as pltpu
from jax.sharding import PartitionSpec as P

LOG2E = math.log2(math.e)
LN2 = math.log(2.0)
ROWS = 16


def split_pieces(value, count):
    pieces = []
    rest = value
    for _ in range(count):
        piece = lax.reduce_precision(rest, 8, 7)
        pieces.append(piece)
        rest = rest - piece
    return pieces


def logsum_kernel(
    keep_ref, inv_ref, theta_ref, end_ref, skim_ref, weight_ref, out_ref, w_scratch, *acc_refs
):
    tables, block_rows, width = skim_ref.shape
    modes = weight_ref.shape[3]
    depth = tables * ROWS
    nests = theta_ref.shape[0]
    row_id = lax.broadcasted_iota(jnp.int32, (ROWS, depth), 0)
    lane_id = lax.broadcasted_iota(jnp.int32, (ROWS, depth), 1)
    diagonal = lax.rem(lane_id, ROWS) == row_id
    groups = block_rows // ROWS
    pair = len(acc_refs)

    def column_block(index, carry):
        cols = pl.ds(pl.multiple_of(index * 128, 128), 128)
        for mode in range(modes):
            for piece in range(4):
                row = weight_ref[0, index, piece, pl.ds(mode, 1), :]
                tile = jnp.broadcast_to(row, (ROWS, depth))
                if piece < 3:
                    tile = jnp.where(diagonal, tile, 0.0)
                w_scratch[mode * ROWS:(mode + 1) * ROWS, piece * depth:(piece + 1) * depth] = (
                    tile.astype(jnp.bfloat16)
                )
        ones = jnp.ones((depth, 128 * pair), jnp.bfloat16)
        for start in range(0, groups, pair):
            parts = []
            for group in range(start, start + pair):
                parts.append(
                    skim_ref[:, group * ROWS:(group + 1) * ROWS, cols].reshape(depth, 128)
                )
            data = jnp.concatenate(parts, axis=1)
            stacked = jnp.concatenate([data, data, data, ones], axis=0)
            util = jnp.dot(w_scratch[...], stacked, preferred_element_type=jnp.float32)
            for offset in range(pair):
                acc_ref = acc_refs[offset]
                part = util[:, offset * 128:(offset + 1) * 128].reshape(modes, ROWS, 128)
                top = part[0]
                for mode in range(1, modes):
                    top = jnp.maximum(top, part[mode])
                acc = None
                for mode in range(modes):
                    term = jnp.exp2((part[mode] - top) * inv_ref[mode])
                    acc = term if acc is None else term + keep_ref[mode] * acc
                    acc_ref[mode] = acc
                total = None
                for nest in range(nests):
                    nest_sum = jnp.maximum(acc_ref[end_ref[nest]], 1.2e-38)
                    value = jnp.exp2(theta_ref[nest] * jnp.log2(nest_sum))
                    total = value if total is None else total + value
                group = start + offset
                out_ref[group * ROWS:(group + 1) * ROWS, cols] = (top + jnp.log2(total)) * LN2
        return carry

    lax.fori_loop(0, width // 128, column_block, 0)


def nest_logsum(skim_part, scale_part, mode_coef, mode_const, nest_theta, mode_nest):
    tables, row_count, col_count = skim_part.shape
    block_rows = row_count // scale_part.shape[1]
    block_cols = col_count // scale_part.shape[2]
    nests = nest_theta.shape[0]
    modes = mode_coef.shape[0]
    depth = tables * ROWS
    mode_ids = jnp.arange(modes)
    before = (mode_nest[None, :] < mode_nest[:, None]) | (
        (mode_nest[None, :] == mode_nest[:, None]) & (mode_ids[None, :] < mode_ids[:, None])
    )
    rank = jnp.sum(before.astype(jnp.int32), axis=1)
    place = rank[None, :] == mode_ids[:, None]
    coef = jnp.sum(jnp.where(place[:, :, None], mode_coef[None], 0.0), axis=1) * LOG2E
    const = jnp.sum(jnp.where(place, mode_const[None], 0.0), axis=1) * LOG2E
    nest = jnp.sum(jnp.where(place, mode_nest[None], 0), axis=1)
    inverse = jnp.sum(
        jnp.where(nest[:, None] == jnp.arange(nests)[None, :], 1.0 / nest_theta[None, :], 0.0), axis=1
    )
    keep = jnp.concatenate([jnp.zeros((1,), jnp.float32), (nest[1:] == nest[:-1]).astype(jnp.float32)])
    ends = jnp.sum((mode_nest[None, :] <= jnp.arange(nests)[:, None]).astype(jnp.int32), axis=1) - 1
    weight = jnp.transpose(scale_part, (1, 2, 0))[:, :, None, :] * coef[None, None]
    pieces = [jnp.repeat(piece, ROWS, axis=-1) for piece in split_pieces(weight, 3)]
    lanes = jnp.arange(depth)[None, :]
    const_piece = jnp.zeros((modes, depth), jnp.float32)
    for index, piece in enumerate(split_pieces(const, 3)):
        const_piece = jnp.where(lanes == index, piece[:, None], const_piece)
    pieces.append(jnp.broadcast_to(const_piece, pieces[0].shape))
    weights = jnp.stack(pieces, axis=2)
    width = min(col_count, 1024)
    per = width // block_cols
    pair = 2
    smem = pl.BlockSpec(memory_space=pltpu.SMEM)
    return pl.pallas_call(
        logsum_kernel,
        grid=(row_count // block_rows, col_count // width),
        out_shape=jax.ShapeDtypeStruct((row_count, col_count), jnp.float32),
        in_specs=[
            smem, smem, smem, smem,
            pl.BlockSpec((tables, block_rows, width), lambda i, j: (0, i, j)),
            pl.BlockSpec((1, per, 4, modes, depth), lambda i, j: (i, j, 0, 0, 0)),
        ],
        out_specs=pl.BlockSpec((block_rows, width), lambda i, j: (i, j)),
        scratch_shapes=[pltpu.VMEM((modes * ROWS, 4 * depth), jnp.bfloat16)]
        + [pltpu.VMEM((modes, ROWS, 128), jnp.float32)] * pair,
        compiler_params=pltpu.CompilerParams(vmem_limit_bytes=40 * 1024 * 1024),
        cost_estimate=pl.CostEstimate(
            flops=200 * row_count * col_count,
            bytes_accessed=(2 * tables + 4) * row_count * col_count,
            transcendentals=21 * row_count * col_count,
        ),
        name="logsum",
    )(keep, inverse, nest_theta, ends, skim_part, weights)


def stats_kernel(zone_ref, count_ref, coef_ref, feat_ref, attr_ref, rows_ref, out_ref, score_ref, lse_ref):
    tours = feat_ref.shape[0]
    tour_size = tours // 8
    step = pl.program_id(0)
    factor = coef_ref[0] * LOG2E
    score_ref[...] = jnp.dot(feat_ref[...], attr_ref[...], preferred_element_type=jnp.float32)
    for block in range(8):
        home = rows_ref[pl.ds(zone_ref[step * 8 + block], 1), :] * factor
        for start in range(0, tour_size, ROWS):
            base = block * tour_size + start

            @pl.when(count_ref[step * 8 + block] > start)
            def _():
                score = score_ref[base:base + ROWS, :] * LOG2E + home
                top = jnp.max(score, axis=1, keepdims=True)
                total = jnp.sum(jnp.exp2(score - top), axis=1, keepdims=True)
                lse_ref[base:base + ROWS, :] = jnp.broadcast_to(top + jnp.log2(total), (ROWS, 128))

    for part in range(tours // 128):
        turned = jnp.transpose(lse_ref[part * 128:(part + 1) * 128, :])
        out_ref[0, part:part + 1, :] = turned[0:1, :]


def trips_kernel(
    zone_ref, count_ref, coef_ref, feat_ref, attr_ref, rows_ref, parts_ref, out_ref, score_ref, bias_ref, *, scale
):
    tours = feat_ref.shape[0]
    tour_size = tours // 8
    step = pl.program_id(0)
    width = out_ref.shape[1]
    factor = coef_ref[0] * LOG2E

    @pl.when(step == 0)
    def _():
        out_ref[...] = jnp.zeros_like(out_ref)

    score_ref[...] = jnp.dot(feat_ref[...], attr_ref[...], preferred_element_type=jnp.float32)
    parts = parts_ref[:, 0]
    top = jnp.max(parts, axis=0)
    lse = top + jnp.log2(jnp.sum(jnp.exp2(parts - top[None]), axis=0))
    for part in range(tours // 128):
        bias_ref[part * 128:(part + 1) * 128, :] = jnp.transpose(
            jnp.broadcast_to(lse[part:part + 1, :], (128, 128))
        )
    row_id = lax.broadcasted_iota(jnp.int32, (ROWS, 128), 0)
    for block in range(8):
        zone = zone_ref[step * 8 + block]
        count = count_ref[step * 8 + block]
        home = rows_ref[pl.ds(zone, 1), :] * factor
        for start in range(0, tour_size, ROWS):
            base = block * tour_size + start

            @pl.when(count > start)
            def _():
                bias = jnp.where(row_id < count - start, bias_ref[base:base + ROWS, :], 1e30)
                wide = jnp.concatenate([bias] * (width // 128), axis=1)
                score = score_ref[base:base + ROWS, :] * LOG2E + home
                total = jnp.sum(jnp.exp2(score - wide), axis=0, keepdims=True)
                out_ref[pl.ds(zone, 1), :] = out_ref[pl.ds(zone, 1), :] + scale * total


def tour_trips(feats, logsums, zones, counts, zone_attr, logsum_coef, scale):
    tours, features = feats.shape
    slots = zones.shape[0]
    anchors, width = logsums.shape
    steps = slots // 8
    group = tours // steps
    smem = pl.BlockSpec(memory_space=pltpu.SMEM)
    once = pl.Buffered(1)
    common = [
        smem, smem, smem,
        pl.BlockSpec((group, features), lambda i: (i, 0)),
        pl.BlockSpec((features, width), lambda i: (0, 0), pipeline_mode=once),
        pl.BlockSpec((anchors, width), lambda i: (0, 0), pipeline_mode=once),
    ]
    params = pltpu.CompilerParams(vmem_limit_bytes=48 * 1024 * 1024)
    lines = group // 128
    local_lse = pl.pallas_call(
        stats_kernel,
        grid=(steps,),
        out_shape=jax.ShapeDtypeStruct((steps, lines, 128), jnp.float32),
        in_specs=common,
        out_specs=pl.BlockSpec((1, lines, 128), lambda i: (i, 0, 0)),
        scratch_shapes=[pltpu.VMEM((group, width), jnp.float32), pltpu.VMEM((group, 128), jnp.float32)],
        compiler_params=params,
        name="stats",
    )(zones, counts, logsum_coef, feats, zone_attr, logsums)
    gathered = lax.all_gather(local_lse, "dest")
    return pl.pallas_call(
        functools.partial(trips_kernel, scale=scale),
        grid=(steps,),
        out_shape=jax.ShapeDtypeStruct((anchors, width), jnp.float32),
        in_specs=common
        + [pl.BlockSpec((gathered.shape[0], 1, lines, 128), lambda i: (0, i, 0, 0))],
        out_specs=pl.BlockSpec((anchors, width), lambda i: (0, 0), pipeline_mode=once),
        scratch_shapes=[pltpu.VMEM((group, width), jnp.float32), pltpu.VMEM((group, 128), jnp.float32)],
        compiler_params=params,
        name="trips",
    )(zones, counts, logsum_coef, feats, zone_attr, logsums, gathered)


def local(
    skim_tables,
    block_scale,
    mode_coef,
    mode_const,
    nest_theta,
    mode_nest,
    logsum_coef,
    tour_attr,
    zone_attr,
    block_zone,
    block_count,
):
    sources = lax.axis_size("orig")
    blocks_here = block_zone.shape[0]
    anchors = skim_tables.shape[1]
    tour_size = tour_attr.shape[0] // blocks_here
    features = tour_attr.shape[1]
    capacity = max(2, 2 * blocks_here // sources)
    slot_count = sources * capacity
    factor = anchors * sources / tour_size
    source_dev = block_zone // anchors
    local_zone = block_zone - source_dev * anchors
    block_ids = jnp.arange(blocks_here)
    same = (source_dev[:, None] == source_dev[None, :]) & (block_ids[None, :] < block_ids[:, None])
    slot_rank = jnp.sum(same.astype(jnp.int32), axis=1)
    slot_of_block = source_dev * capacity + slot_rank
    slot_match = slot_of_block[None, :] == jnp.arange(slot_count)[:, None]
    code = local_zone * 64 + block_count
    send_code = jnp.sum(jnp.where(slot_match, code[None, :], 0), axis=1)
    tour_feats = tour_attr.reshape(blocks_here, tour_size * features)
    send_feats = jnp.dot(slot_match.astype(jnp.bfloat16), tour_feats)
    recv_feats = lax.all_to_all(
        send_feats.reshape(sources, capacity * tour_size, features), "orig", split_axis=0, concat_axis=0, tiled=True
    )
    recv_code = lax.all_to_all(
        send_code.reshape(sources, capacity), "orig", split_axis=0, concat_axis=0, tiled=True
    ).reshape(slot_count)
    logsums = nest_logsum(skim_tables, block_scale, mode_coef, mode_const, nest_theta, mode_nest)
    trip_matrix = tour_trips(
        recv_feats.reshape(slot_count * tour_size, features),
        logsums,
        recv_code // 64,
        recv_code % 64,
        zone_attr,
        logsum_coef,
        factor,
    )
    return (logsums, trip_matrix)


def solution(mesh):
    return jax.shard_map(
        local,
        mesh=mesh,
        in_specs=(
            P(None, "orig", "dest"),
            P(None, "orig", "dest"),
            P(),
            P(),
            P(),
            P(),
            P(),
            P("orig", None),
            P(None, "dest"),
            P("orig"),
            P("orig"),
        ),
        out_specs=(P("orig", "dest"), P("orig", "dest")),
        check_vma=False,
    )
```

```python
import functools
import math

import jax
import jax.numpy as jnp
from jax import lax
from jax.experimental import pallas as pl
from jax.experimental.pallas import tpu as pltpu
from jax.sharding import PartitionSpec as P

LOG2E = math.log2(math.e)
LN2 = math.log(2.0)
ROWS = 16
STEP_BLOCKS = 16
NS = 2


def logsum_kernel(
    keep_ref, inv_ref, theta_ref, end_ref, skim_ref, coef_ref, const_ref, mconst_ref, scale_ref, out_ref, *scratch
):
    tables, block_rows, width = skim_ref.shape
    modes = coef_ref.shape[0]
    nests = theta_ref.shape[0]
    w_refs, acc_refs = scratch[:NW], scratch[NW:]
    rows = HALF
    narrow = tables * rows
    row_id = lax.broadcasted_iota(jnp.int32, (rows, narrow), 0)
    lane_id = lax.broadcasted_iota(jnp.int32, (rows, narrow), 1)
    diagonal = lax.rem(lane_id, rows) == row_id
    groups = block_rows // rows
    pair = PAIR

    def build(index, w_scratch):
        rest = coef_ref[...] * scale_ref[0, pl.ds(index, 1), :]
        pieces = []
        for piece in range(NP):
            rounded = rest.astype(jnp.bfloat16).astype(jnp.float32)
            rest = rest - rounded
            pieces.append(rounded)
        if CONST:
            pieces.append(const_ref[...])
        for mode in range(0, modes, 16 // rows):
            strips = []
            for piece, value in enumerate(pieces):
                tiles = []
                for sub in range(16 // rows):
                    tile = jnp.broadcast_to(value[mode + sub:mode + sub + 1, :], (rows, narrow))
                    tiles.append(jnp.where(diagonal, tile, 0.0) if piece < NP else tile)
                strips.append(tiles[0] if len(tiles) == 1 else jnp.concatenate(tiles, axis=0))
            strip = jnp.concatenate(strips, axis=1).astype(jnp.bfloat16)
            w_scratch[mode * rows:mode * rows + 16, :] = strip

    def multiply(index, w_scratch, start):
        cols = pl.ds(pl.multiple_of(index * 128, 128), 128)
        parts = []
        for group in range(start * rows // ROWS, (start + pair) * rows // ROWS):
            wide = skim_ref[:, group * ROWS:(group + 1) * ROWS, cols].astype(jnp.float32)
            parts.append(wide[:, :rows].reshape(narrow, 128).astype(jnp.bfloat16))
            parts.append(wide[:, rows:].reshape(narrow, 128).astype(jnp.bfloat16))
        data = jnp.concatenate(parts, axis=1)
        pieces = [data] * NP + [jnp.ones((narrow, 128 * pair), jnp.bfloat16)]
        return jnp.dot(w_scratch[...], jnp.concatenate(pieces, axis=0), preferred_element_type=jnp.float32)

    def finish(index, start, util):
        cols = pl.ds(pl.multiple_of(index * 128, 128), 128)
        for offset in range(pair):
            acc_ref = acc_refs[(start + offset) % len(acc_refs)]
            part = util[:, offset * 128:(offset + 1) * 128].reshape(modes, rows, 128)
            top = part[0]
            for mode in range(1, modes):
                top = jnp.maximum(top, part[mode])
            acc = None
            for mode in range(modes):
                term = jnp.exp2((part[mode] - top) * inv_ref[mode])
                acc = term if acc is None else term + keep_ref[mode] * acc
                acc_ref[mode] = acc
            total = None
            for nest in range(nests):
                nest_sum = jnp.maximum(acc_ref[end_ref[nest]], 1.2e-38)
                value = jnp.exp2(theta_ref[nest] * jnp.log(nest_sum))
                total = value if total is None else total + value
            group = start + offset
            out_ref[group * rows:(group + 1) * rows, cols] = top * LN2 + jnp.log(total)

    copies = len(w_refs)

    def column_blocks(index, carry):
        for copy in range(copies):
            build(index * copies + copy, w_refs[copy])
        pending = []
        for copy in range(copies):
            for start in range(0, groups, pair):
                block = index * copies + copy
                pending.append((block, start, multiply(block, w_refs[copy], start)))
                if len(pending) > AHEAD:
                    finish(*pending.pop(0))
        for item in pending:
            finish(*item)
        return carry

    lax.fori_loop(0, width // 128 // copies, column_blocks, 0)


HALF = 8
NP = 3
CONST = True
NW = 2
AHEAD = 1
PAIR = 2
NACC = 8


def nest_logsum(skim_part, scale_part, mode_coef, mode_const, nest_theta, mode_nest):
    tables, row_count, col_count = skim_part.shape
    row_blocks = scale_part.shape[1]
    col_blocks = scale_part.shape[2]
    block_rows = row_count // row_blocks
    block_cols = col_count // col_blocks
    nests = nest_theta.shape[0]
    modes = mode_coef.shape[0]
    depth = tables * HALF
    mode_ids = jnp.arange(modes)
    before = (mode_nest[None, :] < mode_nest[:, None]) | (
        (mode_nest[None, :] == mode_nest[:, None]) & (mode_ids[None, :] < mode_ids[:, None])
    )
    rank = jnp.sum(before.astype(jnp.int32), axis=1)
    place = rank[None, :] == mode_ids[:, None]
    lanes = jnp.arange(depth)
    of_lane = jnp.arange(tables)[:, None] == lanes[None, :] // HALF
    coef = jnp.sum(jnp.where(place[:, :, None], mode_coef[None], 0.0), axis=1) * LOG2E
    coef_wide = jnp.sum(jnp.where(of_lane[None], coef[:, :, None], 0.0), axis=1)
    const = jnp.sum(jnp.where(place, mode_const[None], 0.0), axis=1) * LOG2E
    nest = jnp.sum(jnp.where(place, mode_nest[None], 0), axis=1)
    inverse = jnp.sum(
        jnp.where(nest[:, None] == jnp.arange(nests)[None, :], 1.0 / nest_theta[None, :], 0.0), axis=1
    )
    keep = jnp.concatenate([jnp.zeros((1,), jnp.float32), (nest[1:] == nest[:-1]).astype(jnp.float32)])
    ends = jnp.sum((mode_nest[None, :] <= jnp.arange(nests)[:, None]).astype(jnp.int32), axis=1) - 1
    scale_wide = jnp.sum(jnp.where(of_lane[:, None, None, :], scale_part[:, :, :, None], 0.0), axis=0)
    const_wide = jnp.zeros((modes, depth), jnp.float32)
    rest = const
    for index in range(3):
        piece = lax.reduce_precision(rest, 8, 7)
        rest = rest - piece
        const_wide = jnp.where(lanes[None, :] == index, piece[:, None], const_wide)
    width = min(col_count, 1024)
    per = width // block_cols
    smem = pl.BlockSpec(memory_space=pltpu.SMEM)
    return pl.pallas_call(
        logsum_kernel,
        grid=(row_blocks, col_count // width),
        out_shape=jax.ShapeDtypeStruct((row_count, col_count), jnp.float32),
        in_specs=[
            smem, smem, smem, smem,
            pl.BlockSpec((tables, block_rows, width), lambda i, j: (0, i, j)),
            pl.BlockSpec((modes, depth), lambda i, j: (0, 0)),
            pl.BlockSpec((modes, depth), lambda i, j: (0, 0)),
            smem,
            pl.BlockSpec((1, per, depth), lambda i, j: (i, j, 0)),
        ],
        out_specs=pl.BlockSpec((block_rows, width), lambda i, j: (i, j)),
        scratch_shapes=[pltpu.VMEM((modes * HALF, (NP + CONST) * depth), jnp.bfloat16)] * NW
        + [pltpu.VMEM((modes, HALF, 128), jnp.float32)] * NACC,
        compiler_params=pltpu.CompilerParams(vmem_limit_bytes=40 * 1024 * 1024),
        cost_estimate=pl.CostEstimate(
            flops=200 * row_count * col_count,
            bytes_accessed=(2 * tables + 4) * row_count * col_count,
            transcendentals=21 * row_count * col_count,
        ),
        name="logsum",
    )(keep, inverse, nest_theta * LOG2E, ends, skim_part, coef_wide, const_wide, const, scale_wide)


def stats_kernel(zone_ref, coef_ref, feat_ref, attr_ref, rows_ref, out_ref, top_ref, sum_ref, *score_refs):
    tours = feat_ref.shape[0]
    width = rows_ref.shape[1]
    tour_size = tours // STEP_BLOCKS
    step = pl.program_id(0)
    factor = coef_ref[0] * LOG2E
    half = tours // len(score_refs)
    for index, score_ref in enumerate(score_refs):
        score_ref[...] = jnp.dot(
            feat_ref[index * half:(index + 1) * half, :], attr_ref[...], preferred_element_type=jnp.float32
        )
    for block in range(STEP_BLOCKS):
        home = rows_ref[pl.ds(zone_ref[step * STEP_BLOCKS + block], 1), :] * factor
        for start in range(0, tour_size, ROWS):
            base = block * tour_size + start
            score_ref = score_refs[base // half]
            score = score_ref[base % half:base % half + ROWS, :] * LOG2E + home
            tiles = [score[:, col:col + 128] for col in range(0, width, 128)]
            top = functools.reduce(jnp.maximum, tiles)
            total = functools.reduce(jnp.add, [jnp.exp2(tile - top) for tile in tiles])
            top_ref[base:base + ROWS, :] = top
            sum_ref[base:base + ROWS, :] = total
    for part in range(tours // 128):
        tops = jnp.transpose(top_ref[part * 128:(part + 1) * 128, :])
        sums = jnp.transpose(sum_ref[part * 128:(part + 1) * 128, :])
        top = jnp.max(tops, axis=0, keepdims=True)
        out_ref[0, part:part + 1, :] = top + jnp.log2(jnp.sum(sums * jnp.exp2(tops - top), axis=0, keepdims=True))


def trips_kernel(
    zone_ref, count_ref, coef_ref, feat_ref, attr_ref, rows_ref, parts_ref, out_ref, bias_ref, *score_refs, scale
):
    tours = feat_ref.shape[0]
    tour_size = tours // STEP_BLOCKS
    step = pl.program_id(0)
    width = out_ref.shape[1]
    factor = coef_ref[0] * LOG2E

    @pl.when(step == 0)
    def _():
        out_ref[...] = jnp.zeros_like(out_ref)

    half = tours // len(score_refs)
    for index, score_ref in enumerate(score_refs):
        score_ref[...] = jnp.dot(
            feat_ref[index * half:(index + 1) * half, :], attr_ref[...], preferred_element_type=jnp.float32
        )
    parts = parts_ref[:, 0]
    top = jnp.max(parts, axis=0)
    lse = top + jnp.log2(jnp.sum(jnp.exp2(parts - top[None]), axis=0))
    for part in range(tours // 128):
        bias_ref[part * 128:(part + 1) * 128, :] = jnp.transpose(
            jnp.broadcast_to(lse[part:part + 1, :], (128, 128))
        )
    row_id = lax.broadcasted_iota(jnp.int32, (tour_size, 128), 0)
    for block in range(STEP_BLOCKS):
        zone = zone_ref[step * STEP_BLOCKS + block]
        count = count_ref[step * STEP_BLOCKS + block]
        home = rows_ref[pl.ds(zone, 1), :] * factor
        base = block * tour_size
        bias = jnp.where(row_id < count, bias_ref[base:base + tour_size, :], 1e30)
        totals = []
        for col in range(0, width, 128):
            score = score_refs[base // half][base % half:base % half + tour_size, col:col + 128] * LOG2E + home[:, col:col + 128]
            totals.append(jnp.sum(jnp.exp2(score - bias), axis=0, keepdims=True))
        total = jnp.concatenate(totals, axis=1)
        out_ref[pl.ds(zone, 1), :] = out_ref[pl.ds(zone, 1), :] + scale * total


def tour_trips(feats, logsums, zones, counts, zone_attr, logsum_coef, scale):
    tours, features = feats.shape
    slots = zones.shape[0]
    anchors, width = logsums.shape
    steps = slots // STEP_BLOCKS
    group = tours // steps
    smem = pl.BlockSpec(memory_space=pltpu.SMEM)
    once = pl.Buffered(1)
    common = [
        pl.BlockSpec((group, features), lambda i: (i, 0)),
        pl.BlockSpec((features, width), lambda i: (0, 0), pipeline_mode=once),
        pl.BlockSpec((anchors, width), lambda i: (0, 0), pipeline_mode=once),
    ]
    params = pltpu.CompilerParams(vmem_limit_bytes=48 * 1024 * 1024)
    lines = group // 128
    local_lse = pl.pallas_call(
        stats_kernel,
        grid=(steps,),
        out_shape=jax.ShapeDtypeStruct((steps, lines, 128), jnp.float32),
        in_specs=[smem, smem] + common,
        out_specs=pl.BlockSpec((1, lines, 128), lambda i: (i, 0, 0)),
        scratch_shapes=[
            pltpu.VMEM((group, 128), jnp.float32),
            pltpu.VMEM((group, 128), jnp.float32),
        ]
        + [pltpu.VMEM((group // NS, width), jnp.float32)] * NS,
        compiler_params=params,
        name="stats",
    )(zones, logsum_coef, feats, zone_attr, logsums)
    gathered = lax.all_gather(local_lse, "dest")
    return pl.pallas_call(
        functools.partial(trips_kernel, scale=scale),
        grid=(steps,),
        out_shape=jax.ShapeDtypeStruct((anchors, width), jnp.float32),
        in_specs=[smem, smem, smem] + common
        + [pl.BlockSpec((gathered.shape[0], 1, lines, 128), lambda i: (0, i, 0, 0))],
        out_specs=pl.BlockSpec((anchors, width), lambda i: (0, 0), pipeline_mode=once),
        scratch_shapes=[pltpu.VMEM((group, 128), jnp.float32)]
        + [pltpu.VMEM((group // NS, width), jnp.float32)] * NS,
        compiler_params=params,
        name="trips",
    )(zones, counts, logsum_coef, feats, zone_attr, logsums, gathered)


def local(
    skim_tables,
    block_scale,
    mode_coef,
    mode_const,
    nest_theta,
    mode_nest,
    logsum_coef,
    tour_attr,
    zone_attr,
    block_zone,
    block_count,
):
    sources = lax.axis_size("orig")
    blocks_here = block_zone.shape[0]
    anchors = skim_tables.shape[1]
    tour_size = tour_attr.shape[0] // blocks_here
    features = tour_attr.shape[1]
    capacity = max(2, 2 * blocks_here // sources)
    slot_count = sources * capacity
    factor = anchors * sources / tour_size
    source_dev = block_zone // anchors
    local_zone = block_zone - source_dev * anchors
    block_ids = jnp.arange(blocks_here)
    same = (source_dev[:, None] == source_dev[None, :]) & (block_ids[None, :] < block_ids[:, None])
    slot_rank = jnp.sum(same.astype(jnp.int32), axis=1)
    slot_of_block = source_dev * capacity + slot_rank
    slot_match = slot_of_block[None, :] == jnp.arange(slot_count)[:, None]
    code = local_zone * 64 + block_count
    send_code = jnp.sum(jnp.where(slot_match, code[None, :], 0), axis=1)
    tour_feats = tour_attr.reshape(blocks_here, tour_size * features)
    send_feats = jnp.dot(slot_match.astype(jnp.bfloat16), tour_feats)
    recv_feats = lax.all_to_all(
        send_feats.reshape(sources, capacity * tour_size, features), "orig", split_axis=0, concat_axis=0, tiled=True
    )
    recv_code = lax.all_to_all(
        send_code.reshape(sources, capacity), "orig", split_axis=0, concat_axis=0, tiled=True
    ).reshape(slot_count)
    logsums = nest_logsum(skim_tables, block_scale, mode_coef, mode_const, nest_theta, mode_nest)
    trip_matrix = tour_trips(
        recv_feats.reshape(slot_count * tour_size, features),
        logsums,
        recv_code // 64,
        recv_code % 64,
        zone_attr,
        logsum_coef,
        factor,
    )
    return (logsums, trip_matrix)


def solution(mesh):
    return jax.shard_map(
        local,
        mesh=mesh,
        in_specs=(
            P(None, "orig", "dest"),
            P(None, "orig", "dest"),
            P(),
            P(),
            P(),
            P(),
            P(),
            P("orig", None),
            P(None, "dest"),
            P("orig"),
            P("orig"),
        ),
        out_specs=(P("orig", "dest"), P("orig", "dest")),
        check_vma=False,
    )
```
